32 devices in a mesh: chan: 16 (over z, y, x), pos: 2 (over core).
Axes of the slice: x: 2, y: 2, z: 4, core: 2. Of those that a mesh axis runs over, the one named last changes fastest.
Arguments:
- patches: bfloat16 [16, 2, 512, 256], P(None, 'pos', 'chan'), may hold values from -30 to 30
- tok_weight: bfloat16 [32, 256, 1024], P('chan'), may hold values from -2 to 2
- mixing: bfloat16 [32, 16, 16], P('chan'), may hold values from -1.5 to 1.5
- chan_embed: bfloat16 [512, 1024], P('chan'), may hold values from -3 to 3
- norm_gain: float32 [1024], replicated, may hold values from 0.5 to 1.5
- qkv_weight: bfloat16 [1024, 3072], replicated, may hold values from -8 to 8
- upstream: bfloat16 [16, 2, 512, 1024], P(None, 'pos', 'chan'), may hold values from -6 to 6
Outputs:
- encoded: bfloat16 [16, 2, 512, 1024], P(None, 'pos', 'chan')
- tok_grad: float32 [2, 32, 256, 1024], P('pos', 'chan')
- mix_grad: float32 [32, 16, 16], P('chan')
- embed_grad: float32 [512, 1024], P('chan')
The draws below stay inside these ranges and needn't reach their ends.
All inputs are finite; a program needn't handle non-finite values.
Results may differ from the reference program's by a relative error of at most 0.006.
The reference program's roundings to bfloat16 on the way count: a program that leaves them out, or rounds other values in their place, can miss the bound.
Values may be sent and summed in bfloat16 or wider, within the bound.
A program may use at most 128 MiB of HBM per device.

```python
import math
import jax
import jax.numpy as jnp
from jax import lax

C = 512
GROUP = 16
PIX = 256
D = 1024
HEADS = 8
HDIM = 128
GROUPS = 32
ROWS = 16
COLS = 2


def draw_patches(key, part):
    key_scale, key_own = jax.random.split(key, 2)
    chan_scale = jnp.exp(jax.random.uniform(key_scale, (1, 1, C, 1), jnp.float32, math.log(0.3), math.log(3.0)))
    drawn = jax.random.normal(key_own, (ROWS, COLS, C, PIX), jnp.float32) * chan_scale
    return jnp.clip(drawn, -30.0, 30.0).astype(jnp.bfloat16)


def draw_tok_weight(key, part):
    key_column, key_entry = jax.random.split(key, 2)
    column_scale = jnp.exp(jax.random.uniform(key_column, (GROUPS, 1, D), jnp.float32, math.log(0.3), math.log(3.0)))
    entries = jax.random.normal(key_entry, (GROUPS, PIX, D), jnp.float32)
    drawn = entries * column_scale / math.sqrt(PIX)
    return jnp.clip(drawn, -2.0, 2.0).astype(jnp.bfloat16)


def draw_qkv_weight(key, part):
    key_query, key_key, key_value = jax.random.split(key, 3)
    w_query = jax.random.normal(key_query, (D, D), jnp.float32) / math.sqrt(D)
    w_key = jax.random.normal(key_key, (D, D), jnp.float32) / math.sqrt(D)
    w_value = jax.random.normal(key_value, (D, D), jnp.float32) / math.sqrt(D)
    drawn = jnp.concatenate([w_query, w_key, w_value], axis=1)
    return jnp.clip(drawn, -8.0, 8.0).astype(jnp.bfloat16)


def block_levels(key, dims, pieces, smallest, top_value):
    level = 1.0
    for dim, blocks in pieces:
        heights = jax.random.uniform(jax.random.fold_in(jax.random.fold_in(key, 6), dim), (blocks,), jnp.float32, smallest / len(pieces), top_value / len(pieces))
        level = level * jnp.repeat(jnp.exp(heights), dims[dim] // blocks).reshape((-1,) + (1,) * (len(dims) - 1 - dim))
    return level


def scatter_about(rng, shape, scale, limit, pieces=(), held_as=jnp.bfloat16):
    factor_of = block_levels(rng, shape, pieces, -0.22, 0.18) if pieces else 1.0
    result = jax.random.normal(rng, shape, jnp.float32) * scale * factor_of
    return jnp.minimum(jnp.maximum(result, -limit), limit).astype(held_as)


def setup_inputs(seed: int = 0) -> dict:
    keys = jax.random.split(jax.random.key(seed), 8)
    patches = draw_patches(jax.random.fold_in(keys[7], 71), 0)
    tok_weight = draw_tok_weight(jax.random.fold_in(keys[7], 71), 0)
    mixing = scatter_about(keys[2], (GROUPS, GROUP, GROUP), GROUP ** -0.5, 1.5, ((0, 16),))
    chan_embed = scatter_about(keys[3], (C, D), 0.5, 3.0, ((0, 16),))
    norm_gain = jnp.clip(1.0 + 0.1 * jax.random.normal(keys[4], (D,), jnp.float32), 0.5, 1.5)
    qkv_weight = draw_qkv_weight(jax.random.fold_in(keys[7], 71), 0)
    upstream = scatter_about(keys[6], (ROWS, COLS, C, D), 1.0, 6.0, ((1, 2), (2, 16)))
    return dict(patches=patches, tok_weight=tok_weight, mixing=mixing, chan_embed=chan_embed, norm_gain=norm_gain, qkv_weight=qkv_weight, upstream=upstream)


HIGH = lax.Precision.HIGHEST

def attend_forward(mixed, qkv_weight, norm_gain):
    count, chans, width = mixed.shape
    mixed_f = mixed.astype(jnp.float32)
    inv_rms = lax.rsqrt(lax.optimization_barrier(jnp.mean(mixed_f * mixed_f, axis=-1, keepdims=True)) + 1e-06)
    normed = (mixed_f * inv_rms * norm_gain).astype(jnp.bfloat16)
    projected = jnp.dot(normed.reshape(count * chans, width), qkv_weight, preferred_element_type=jnp.float32)
    projected = projected.astype(jnp.bfloat16).reshape(count, chans, 3, HEADS, HDIM)
    queries = projected[:, :, 0]
    key_rows = projected[:, :, 1]
    values = projected[:, :, 2]
    score_scale = 1.0 / math.sqrt(HDIM)
    scores = jnp.einsum('pchd,pehd->phce', queries.astype(jnp.float32), key_rows.astype(jnp.float32), precision=HIGH) * score_scale
    row_max = lax.optimization_barrier(jnp.max(scores, axis=-1, keepdims=True))
    exp_scores = jnp.exp(scores - row_max)
    attn_probs = exp_scores / lax.optimization_barrier(jnp.sum(exp_scores, axis=-1, keepdims=True))
    probs_low = attn_probs.astype(jnp.bfloat16)
    attended = jnp.einsum('phce,pehd->pchd', probs_low.astype(jnp.float32), values.astype(jnp.float32), precision=HIGH)
    attended = attended.reshape(count, chans, width).astype(jnp.bfloat16)
    return (attended, (mixed_f, inv_rms, queries, key_rows, values, attn_probs, probs_low))

def attend_backward(saved, upstream_rows, qkv_weight, norm_gain):
    mixed_f, inv_rms, queries, key_rows, values, attn_probs, probs_low = saved
    count, chans, width = mixed_f.shape
    score_scale = 1.0 / math.sqrt(HDIM)
    grad_out = upstream_rows.reshape(count, chans, HEADS, HDIM).astype(jnp.float32)
    grad_probs = jnp.einsum('pchd,pehd->phce', grad_out, values.astype(jnp.float32), precision=HIGH)
    grad_values = jnp.einsum('phce,pchd->pehd', probs_low.astype(jnp.float32), grad_out, precision=HIGH)
    inner = lax.optimization_barrier(jnp.sum(attn_probs * grad_probs, axis=-1, keepdims=True))
    grad_scores = (attn_probs * (grad_probs - inner) * score_scale).astype(jnp.bfloat16).astype(jnp.float32)
    grad_queries = jnp.einsum('phce,pehd->pchd', grad_scores, key_rows.astype(jnp.float32), precision=HIGH)
    grad_keys = jnp.einsum('phce,pchd->pehd', grad_scores, queries.astype(jnp.float32), precision=HIGH)
    grad_projected = jnp.stack([grad_queries, grad_keys, grad_values], axis=2).astype(jnp.bfloat16)
    grad_projected = grad_projected.reshape(count * chans, 3 * width)
    grad_normed = jnp.dot(grad_projected, qkv_weight.T, preferred_element_type=jnp.float32).reshape(count, chans, width)
    scaled = grad_normed * norm_gain
    grad_branch = inv_rms * (scaled - mixed_f * inv_rms * inv_rms * lax.optimization_barrier(jnp.mean(scaled * mixed_f, axis=-1, keepdims=True)))
    return grad_branch.astype(jnp.bfloat16)

def reference(patches, tok_weight, mixing, chan_embed, norm_gain, qkv_weight, upstream):
    mixing_f = mixing.astype(jnp.float32)
    embed_f = chan_embed.astype(jnp.float32).reshape(GROUPS, GROUP, D)
    weight_f = tok_weight.astype(jnp.float32)

    def column(inputs):
        pix_col, up_col = inputs
        pix_groups = pix_col.reshape(ROWS, GROUPS, GROUP, PIX).astype(jnp.float32)
        tokens = jnp.einsum('rgcp,gpd->rgcd', pix_groups, weight_f, precision=HIGH).astype(jnp.bfloat16)
        mixed = jnp.einsum('gcf,rgfd->rgcd', mixing_f, tokens.astype(jnp.float32), precision=HIGH) + embed_f
        mixed = mixed.astype(jnp.bfloat16).reshape(ROWS, C, D)

        def position(pair):
            mixed_row, up_row = pair
            attended, saved = attend_forward(mixed_row[None], qkv_weight, norm_gain)
            grad_branch = attend_backward(saved, up_row[None], qkv_weight, norm_gain)
            return (attended[0], grad_branch[0])
        attended, grad_branch = lax.map(position, (mixed, up_col))
        encoded = (mixed.astype(jnp.float32) + attended.astype(jnp.float32)).astype(jnp.bfloat16)
        grad_mixed = (up_col.astype(jnp.float32) + grad_branch.astype(jnp.float32)).reshape(ROWS, GROUPS, GROUP, D)
        grad_tokens = jnp.einsum('gcf,rgcd->rgfd', mixing_f, grad_mixed, precision=HIGH).astype(jnp.bfloat16)
        col_tok = jnp.einsum('rgcp,rgcd->gpd', pix_groups, grad_tokens.astype(jnp.float32), precision=HIGH)
        col_mix = jnp.einsum('rgcd,rgfd->gcf', grad_mixed, tokens.astype(jnp.float32), precision=HIGH)
        col_embed = lax.optimization_barrier(jnp.sum(grad_mixed, axis=0)).reshape(C, D)
        return (encoded, col_tok, col_mix, col_embed)
    pix_cols = jnp.swapaxes(patches, 0, 1)
    up_cols = jnp.swapaxes(upstream, 0, 1)
    encoded, tok_grad, mix_parts, embed_parts = lax.map(column, (pix_cols, up_cols))
    return (jnp.swapaxes(encoded, 0, 1), tok_grad, lax.optimization_barrier(jnp.sum(mix_parts, axis=0)), lax.optimization_barrier(jnp.sum(embed_parts, axis=0)))
```

```python
import functools
import math

import jax
import jax.numpy as jnp
from jax import lax
from jax.experimental import pallas as pl
from jax.experimental.pallas import tpu as pltpu
from jax.sharding import PartitionSpec as P

HDIM = 128
F32 = jnp.float32
BF16 = jnp.bfloat16
HIGH = lax.Precision.HIGHEST


def dot(a, b, ca=1, cb=0):
    return lax.dot_general(a, b, (((ca,), (cb,)), ((), ())), preferred_element_type=F32)


def kernel(
    n, npos,
    patches, tokw, mixing, embed, gain, w_hbm, up_hbm,
    enc_out, tok_out, mix_out, emb_out,
    tokens, mixed, mixp, upp, upl, w, proj, probs, inv, encs, gproj, gn, gbs, gbr,
    emb_all, mix_all, gtok, emb_up,
    s1, r1, s2, r2, s3, r3, s4, r4, se, re, sm, rm, lsem,
):
    me = lax.axis_index("chan")
    mypos = lax.axis_index("pos")
    rows, _, cc, pix = patches.shape
    groups, group, _ = mixing.shape
    width = embed.shape[1]
    chans = n * cc
    heads = width // HDIM

    barrier = pltpu.get_barrier_semaphore()

    def greet(d, c):
        pl.semaphore_signal(barrier, inc=1, device_id={"chan": lax.rem(me + d, n)})
        return c

    lax.fori_loop(1, n, greet, 0)

    def greet_pos(q, c):
        pl.semaphore_signal(barrier, inc=1, device_id={"pos": lax.rem(mypos + q, npos)})
        return c

    lax.fori_loop(1, npos, greet_pos, 0)

    w_copy = pltpu.make_async_copy(w_hbm, w, lsem.at[0])
    up_copy = pltpu.make_async_copy(up_hbm.at[:, 0], upl, lsem.at[1])
    own_up = pltpu.make_async_copy(up_hbm.at[me, 0], upp.at[me], lsem.at[2])
    up_copy.start()
    own_up.start()
    w_copy.start()

    def remote(src, dst, ss, rs, d, peer):
        return pltpu.make_async_remote_copy(
            src_ref=src, dst_ref=dst, send_sem=ss.at[d], recv_sem=rs.at[d], device_id={"chan": peer}
        )

    long = rows * group
    pick = (lax.broadcasted_iota(jnp.int32, (long, group), 0) % group
            == lax.broadcasted_iota(jnp.int32, (long, group), 1))
    pick_f = pick.astype(F32)
    same = (lax.broadcasted_iota(jnp.int32, (long, long), 0) // group
            == lax.broadcasted_iota(jnp.int32, (long, long), 1) // group)

    def block_diag(g):
        tall = dot(pick_f.astype(BF16), mixing[g]).astype(BF16)
        full = dot(tall, pick_f.astype(BF16), 1, 1)
        return jnp.where(same, full, 0.0).astype(BF16)

    for g in range(groups):
        ch = slice(g * group, (g + 1) * group)
        pg = patches[:, 0, ch, :].reshape(long, pix)
        tok = dot(pg, tokw[g]).astype(BF16)
        tokens[g] = tok
        mix = dot(block_diag(g), tok).reshape(rows, group, width) + embed[ch, :].astype(F32)[None]
        mixed[:, ch, :] = mix.astype(BF16)

    pl.semaphore_wait(barrier, n - 1 + npos - 1)

    def send1(d, c):
        peer = lax.rem(me + d, n)
        remote(mixed.at[peer], mixp.at[me], s1, r1, d, peer).start()
        return c

    lax.fori_loop(1, n, send1, 0)

    def send2(d, c):
        peer = lax.rem(me + d, n)
        remote(up_hbm.at[peer, 0], upp.at[me], s2, r2, d, peer).start()
        return c

    lax.fori_loop(1, n, send2, 0)

    mixp[pl.ds(me, 1)] = mixed[pl.ds(me, 1)]

    up_copy.wait()
    for g in range(groups):
        ch = slice(g * group, (g + 1) * group)
        ug = upl[:, ch, :].reshape(long, width)
        gtok[g] = dot(block_diag(g), ug, 0, 0)
        prod = jnp.where(same, dot(ug, tokens[g], 1, 1), 0.0)
        wide = jnp.sum(prod.reshape(rows, group, long), axis=0)
        mix_out[g] = jnp.dot(wide, pick_f, precision=HIGH, preferred_element_type=F32)
        emb_up[ch, :] = jnp.sum(upl[:, ch, :].astype(F32), axis=0)

    def recv1(d, c):
        src = lax.rem(me + n - d, n)
        remote(mixed.at[src], mixp.at[src], s1, r1, d, src).wait_recv()
        return c

    lax.fori_loop(1, n, recv1, 0)
    w_copy.wait()

    x = mixp[...].reshape(chans, width).astype(F32)
    ir = lax.rsqrt(jnp.mean(x * x, axis=-1, keepdims=True) + 1e-06)
    inv[...] = ir
    gbs[...] = (x * ir * gain[...]).astype(BF16).reshape(n, cc, width)

    span = 512
    half = chans // 2

    def project(k, c):
        cols = pl.ds(pl.multiple_of(k * span, span), span)
        proj[:, cols] = dot(gbs[...].reshape(chans, width), w[:, cols]).astype(BF16)
        return c

    lax.fori_loop(0, 3 * width // span, project, 0)

    scale = 1.0 / math.sqrt(HDIM)
    fold = scale / math.log(2.0)

    def head_cols(h, part):
        return pl.ds(pl.multiple_of(part * width + h * HDIM, HDIM), HDIM)

    def forward(h, c):
        q, k, v = (proj[:, head_cols(h, part)] for part in range(3))
        s = dot(q, k, 1, 1)
        e = jnp.exp2((s - jnp.max(s, axis=-1, keepdims=True)) * fold)
        p = e * (1.0 / jnp.sum(e, axis=-1, keepdims=True))
        probs[pl.ds(h, 1)] = p[None]
        cols = head_cols(h, 0)
        att = dot(p.astype(BF16), v).astype(BF16)
        m = mixp[:, :, cols].astype(F32)
        encs[:, :, cols] = (m + att.reshape(n, cc, HDIM).astype(F32)).astype(BF16)
        return c

    lax.fori_loop(0, heads, forward, 0)

    def send3(d, c):
        peer = lax.rem(me + d, n)
        remote(encs.at[peer], enc_out.at[me, 0], s3, r3, d, peer).start()
        return c

    lax.fori_loop(1, n, send3, 0)
    own_enc = pltpu.make_async_copy(encs.at[me], enc_out.at[me, 0], lsem.at[3])
    own_enc.start()

    own_up.wait()

    def recv2(d, c):
        src = lax.rem(me + n - d, n)
        remote(up_hbm.at[src, 0], upp.at[src], s2, r2, d, src).wait_recv()
        return c

    lax.fori_loop(1, n, recv2, 0)

    def backward(h, c):
        q, k, v = (proj[:, head_cols(h, part)] for part in range(3))
        do = upp[:, :, head_cols(h, 0)].reshape(chans, HDIM)
        p = probs[pl.ds(h, 1)][0]
        dp = dot(do, v, 1, 1)
        gproj[:, head_cols(h, 2)] = dot(p.astype(BF16), do, 0, 0).astype(BF16)
        inner = jnp.sum(p * dp, axis=-1, keepdims=True)
        ds = (p * (dp - inner) * scale).astype(BF16)
        gproj[:, head_cols(h, 0)] = dot(ds, k).astype(BF16)
        gproj[:, head_cols(h, 1)] = dot(ds, q, 0, 0).astype(BF16)
        return c

    lax.fori_loop(0, heads, backward, 0)

    per = n // 2
    wide_cols = 256

    def finish(b, c):
        rs = pl.ds(pl.multiple_of(b * half, half), half)

        def back_project(k, c2):
            cols = pl.ds(pl.multiple_of(k * wide_cols, wide_cols), wide_cols)
            gn[:, cols] = dot(gproj[rs, :], w[cols, :], 1, 1)
            return c2

        lax.fori_loop(0, width // wide_cols, back_project, 0)
        scaled = gn[...] * gain[...]
        xb = mixp[pl.ds(b * per, per)].reshape(half, width).astype(F32)
        ib = inv[rs, :]
        mean = jnp.mean(scaled * xb, axis=-1, keepdims=True)
        gb = ib * (scaled - xb * ib * ib * mean)
        gbs[pl.ds(b * per, per)] = gb.astype(BF16).reshape(per, cc, width)

        def send4(j, c2):
            peer = b * per + j
            d = lax.rem(peer + n - me, n)

            @pl.when(peer != me)
            def _():
                remote(gbs.at[peer], gbr.at[me], s4, r4, d, peer).start()

            return c2

        lax.fori_loop(0, per, send4, 0)
        return c

    lax.fori_loop(0, 2, finish, 0)
    gbr[pl.ds(me, 1)] = gbs[pl.ds(me, 1)]

    def recv4(d, c):
        src = lax.rem(me + n - d, n)
        remote(gbs.at[src], gbr.at[src], s4, r4, d, src).wait_recv()
        return c

    lax.fori_loop(1, n, recv4, 0)

    for g in range(groups):
        ch = slice(g * group, (g + 1) * group)
        gb = gbr[:, ch, :]
        emb = emb_up[ch, :] + jnp.sum(gb.astype(F32), axis=0)
        emb_all[pl.ds(mypos, 1), ch, :] = emb[None]
        gg = gb.reshape(long, width)
        prod = jnp.where(same, dot(gg, tokens[g], 1, 1), 0.0)
        wide = jnp.sum(prod.reshape(rows, group, long), axis=0)
        mg = mix_out[g] + jnp.dot(wide, pick_f, precision=HIGH, preferred_element_type=F32)
        mg = jnp.concatenate([mg, jnp.zeros((group, 128 - group), F32)], axis=1)
        mix_all[pl.ds(mypos, 1), ch, :] = mg[None]

    def pos_copy(ref, ss, rs, q, slot, partner):
        return pltpu.make_async_remote_copy(
            src_ref=ref.at[slot], dst_ref=ref.at[slot], send_sem=ss.at[q], recv_sem=rs.at[q],
            device_id={"pos": partner},
        )

    def send_pos(q, c):
        partner = lax.rem(mypos + q, npos)
        pos_copy(emb_all, se, re, q, mypos, partner).start()
        pos_copy(mix_all, sm, rm, q, mypos, partner).start()
        return c

    lax.fori_loop(1, npos, send_pos, 0)

    for g in range(groups):
        ch = slice(g * group, (g + 1) * group)
        gg = gbr[:, ch, :].reshape(long, width)
        gt = (gtok[g] + dot(block_diag(g), gg, 0, 0)).astype(BF16)
        pg = patches[:, 0, ch, :].reshape(long, pix)
        tok_out[0, g] = dot(pg, gt, 0, 0)

    def recv_pos(q, c):
        src = lax.rem(mypos + npos - q, npos)
        pos_copy(emb_all, se, re, q, src, src).wait_recv()
        pos_copy(mix_all, sm, rm, q, src, src).wait_recv()
        return c

    lax.fori_loop(1, npos, recv_pos, 0)
    emb_out[...] = jnp.sum(emb_all[...], axis=0)
    mix_sum = jnp.sum(mix_all[...], axis=0)
    for g in range(groups):
        mix_out[g] = mix_sum[g * group:(g + 1) * group, :group]

    own_enc.wait()

    def drain(d, c):
        peer = lax.rem(me + d, n)
        src = lax.rem(me + n - d, n)
        remote(encs.at[src], enc_out.at[src, 0], s3, r3, d, src).wait_recv()
        remote(mixed.at[peer], mixp.at[me], s1, r1, d, peer).wait_send()
        remote(up_hbm.at[peer, 0], upp.at[me], s2, r2, d, peer).wait_send()
        remote(encs.at[peer], enc_out.at[me, 0], s3, r3, d, peer).wait_send()
        remote(gbs.at[peer], gbr.at[me], s4, r4, d, peer).wait_send()
        return c

    lax.fori_loop(1, n, drain, 0)

    def drain_pos(q, c):
        partner = lax.rem(mypos + q, npos)
        pos_copy(emb_all, se, re, q, mypos, partner).wait_send()
        pos_copy(mix_all, sm, rm, q, mypos, partner).wait_send()
        return c

    lax.fori_loop(1, npos, drain_pos, 0)


def local(n, npos, patches, tok_weight, mixing, chan_embed, norm_gain, qkv_weight, upstream):
    rows, _, cc, _ = patches.shape
    groups, pix, width = tok_weight.shape
    group = mixing.shape[1]
    chans = n * cc
    heads = width // HDIM
    vm = functools.partial(pl.BlockSpec, memory_space=pltpu.VMEM)
    anyspace = pl.BlockSpec(memory_space=pl.ANY)
    dma = pltpu.SemaphoreType.DMA
    out_shape = (
        jax.ShapeDtypeStruct((rows, 1, cc, width), BF16),
        jax.ShapeDtypeStruct((1, groups, pix, width), F32),
        jax.ShapeDtypeStruct((groups, group, group), F32),
        jax.ShapeDtypeStruct((cc, width), F32),
    )
    block = pltpu.VMEM((n, cc, width), BF16)
    scratch = [
        pltpu.VMEM((groups, rows * group, width), BF16),
        block, block, block, block,
        pltpu.VMEM(qkv_weight.shape, BF16),
        pltpu.VMEM((chans, 3 * width), BF16),
        pltpu.VMEM((heads, chans, chans), F32),
        pltpu.VMEM((chans, 1), F32),
        block,
        pltpu.VMEM((chans, 3 * width), BF16),
        pltpu.VMEM((chans // 2, width), F32),
        block, block,
        pltpu.VMEM((npos, cc, width), F32),
        pltpu.VMEM((npos, groups * group, 128), F32),
        pltpu.VMEM((groups, rows * group, width), F32),
        pltpu.VMEM((cc, width), F32),
    ] + [dma((n,))] * 8 + [dma((npos,))] * 4 + [dma((4,))]
    return pl.pallas_call(
        functools.partial(kernel, n, npos),
        out_shape=out_shape,
        in_specs=[vm()] * 5 + [anyspace] * 2,
        out_specs=(anyspace, vm(), vm(), vm()),
        scratch_shapes=scratch,
        compiler_params=pltpu.CompilerParams(
            collective_id=0, has_side_effects=True, vmem_limit_bytes=56 * 1024 * 1024
        ),
    )(patches, tok_weight, mixing, chan_embed, norm_gain.reshape(1, width), qkv_weight, upstream)


def solution(mesh):
    in_specs = (
        P(None, "pos", "chan", None),
        P("chan", None, None),
        P("chan", None, None),
        P("chan", None),
        P(),
        P(),
        P(None, "pos", "chan", None),
    )
    out_specs = (
        P(None, "pos", "chan", None),
        P("pos", "chan", None, None),
        P("chan", None, None),
        P("chan", None),
    )
    body = functools.partial(local, mesh.shape["chan"], mesh.shape["pos"])
    return jax.shard_map(body, mesh=mesh, in_specs=in_specs, out_specs=out_specs, check_vma=False)
```

```python
import functools
import math

import jax
import jax.numpy as jnp
from jax import lax
from jax.experimental import pallas as pl
from jax.experimental.pallas import tpu as pltpu
from jax.sharding import PartitionSpec as P

HDIM = 128
F32 = jnp.float32
BF16 = jnp.bfloat16
HIGH = lax.Precision.HIGHEST


def dot(a, b, ca=1, cb=0):
    return lax.dot_general(a, b, (((ca,), (cb,)), ((), ())), preferred_element_type=F32)


def kernel(
    n, npos,
    patches, tokw, mixing, embed, gain, w_hbm, up_hbm,
    enc_out, tok_out, mix_out, emb_out,
    tokens, mixed, mixp, upp, upl, w, proj, probs, inv, encs, gproj, gn, gbs, gbr,
    emb_all, mix_all, gtok, emb_up,
    s1, r1, s2, r2, s3, r3, s4, r4, se, re, sm, rm, lsem,
):
    me = lax.axis_index("chan")
    mypos = lax.axis_index("pos")
    rows, _, cc, pix = patches.shape
    groups, group, _ = mixing.shape
    width = embed.shape[1]
    chans = n * cc
    heads = width // HDIM

    barrier = pltpu.get_barrier_semaphore()

    def greet(d, c):
        pl.semaphore_signal(barrier, inc=1, device_id={"chan": lax.rem(me + d, n)})
        return c

    lax.fori_loop(1, n, greet, 0)

    def greet_pos(q, c):
        pl.semaphore_signal(barrier, inc=1, device_id={"pos": lax.rem(mypos + q, npos)})
        return c

    lax.fori_loop(1, npos, greet_pos, 0)

    w_copy = pltpu.make_async_copy(w_hbm, w, lsem.at[0])
    up_copy = pltpu.make_async_copy(up_hbm.at[:, 0], upl, lsem.at[1])
    own_up = pltpu.make_async_copy(up_hbm.at[me, 0], upp.at[me], lsem.at[2])
    up_copy.start()
    own_up.start()
    w_copy.start()

    def remote(src, dst, ss, rs, d, peer):
        return pltpu.make_async_remote_copy(
            src_ref=src, dst_ref=dst, send_sem=ss.at[d], recv_sem=rs.at[d], device_id={"chan": peer}
        )

    long = rows * group
    pick = (lax.broadcasted_iota(jnp.int32, (long, group), 0) % group
            == lax.broadcasted_iota(jnp.int32, (long, group), 1))
    pick_f = pick.astype(F32)
    same = (lax.broadcasted_iota(jnp.int32, (long, long), 0) // group
            == lax.broadcasted_iota(jnp.int32, (long, long), 1) // group)

    def block_diag(g):
        tall = dot(pick_f.astype(BF16), mixing[g]).astype(BF16)
        full = dot(tall, pick_f.astype(BF16), 1, 1)
        return jnp.where(same, full, 0.0).astype(BF16)

    for g in range(groups):
        ch = slice(g * group, (g + 1) * group)
        pg = patches[:, 0, ch, :].reshape(long, pix)
        tok = dot(pg, tokw[g]).astype(BF16)
        tokens[g] = tok
        mix = dot(block_diag(g), tok).reshape(rows, group, width) + embed[ch, :].astype(F32)[None]
        mixed[:, ch, :] = mix.astype(BF16)

    pl.semaphore_wait(barrier, n - 1 + npos - 1)

    def send1(i, c):
        d = n - i
        peer = lax.rem(me + d, n)
        remote(mixed.at[peer], mixp.at[me], s1, r1, d, peer).start()
        return c

    lax.fori_loop(1, n, send1, 0)

    def send2(i, c):
        d = n - i
        peer = lax.rem(me + d, n)
        remote(up_hbm.at[peer, 0], upp.at[me], s2, r2, d, peer).start()
        return c

    lax.fori_loop(1, n, send2, 0)

    mixp[pl.ds(me, 1)] = mixed[pl.ds(me, 1)]

    up_copy.wait()
    for g in range(groups):
        ch = slice(g * group, (g + 1) * group)
        ug = upl[:, ch, :].reshape(long, width)
        gtok[g] = dot(block_diag(g), ug, 0, 0)
        prod = jnp.where(same, dot(ug, tokens[g], 1, 1), 0.0)
        wide = jnp.sum(prod.reshape(rows, group, long), axis=0)
        mix_out[g] = jnp.dot(wide, pick_f, precision=HIGH, preferred_element_type=F32)
        emb_up[ch, :] = jnp.sum(upl[:, ch, :].astype(F32), axis=0)

    def recv1(d, c):
        src = lax.rem(me + n - d, n)
        remote(mixed.at[src], mixp.at[src], s1, r1, d, src).wait_recv()
        return c

    lax.fori_loop(1, n, recv1, 0)
    w_copy.wait()

    x = mixp[...].reshape(chans, width).astype(F32)
    ir = lax.rsqrt(jnp.mean(x * x, axis=-1, keepdims=True) + 1e-06)
    inv[...] = ir
    gbs[...] = (x * ir * gain[...]).astype(BF16).reshape(n, cc, width)

    span = 512
    half = chans // 2

    def project(k, c):
        cols = pl.ds(pl.multiple_of(k * span, span), span)
        proj[:, cols] = dot(gbs[...].reshape(chans, width), w[:, cols]).astype(BF16)
        return c

    lax.fori_loop(0, 3 * width // span, project, 0)

    scale = 1.0 / math.sqrt(HDIM)
    fold = scale / math.log(2.0)

    def head_cols(h, part):
        return pl.ds(pl.multiple_of(part * width + h * HDIM, HDIM), HDIM)

    def forward(h, c):
        q, k, v = (proj[:, head_cols(h, part)] for part in range(3))
        s = dot(q, k, 1, 1)
        e = jnp.exp2((s - jnp.max(s, axis=-1, keepdims=True)) * fold)
        p = e * (1.0 / jnp.sum(e, axis=-1, keepdims=True))
        probs[pl.ds(h, 1)] = p[None]
        cols = head_cols(h, 0)
        att = dot(p.astype(BF16), v).astype(BF16)
        m = mixp[:, :, cols].astype(F32)
        encs[:, :, cols] = (m + att.reshape(n, cc, HDIM).astype(F32)).astype(BF16)
        return c

    lax.fori_loop(0, heads, forward, 0)

    def send3(i, c):
        d = n - i
        peer = lax.rem(me + d, n)
        remote(encs.at[peer], enc_out.at[me, 0], s3, r3, d, peer).start()
        return c

    lax.fori_loop(1, n, send3, 0)
    own_enc = pltpu.make_async_copy(encs.at[me], enc_out.at[me, 0], lsem.at[3])
    own_enc.start()

    own_up.wait()

    def recv2(d, c):
        src = lax.rem(me + n - d, n)
        remote(up_hbm.at[src, 0], upp.at[src], s2, r2, d, src).wait_recv()
        return c

    lax.fori_loop(1, n, recv2, 0)

    def backward(h, c):
        q, k, v = (proj[:, head_cols(h, part)] for part in range(3))
        do = upp[:, :, head_cols(h, 0)].reshape(chans, HDIM)
        p = probs[pl.ds(h, 1)][0]
        dp = dot(do, v, 1, 1)
        gproj[:, head_cols(h, 2)] = dot(p.astype(BF16), do, 0, 0).astype(BF16)
        inner = jnp.sum(p * dp, axis=-1, keepdims=True)
        ds = (p * (dp - inner) * scale).astype(BF16)
        gproj[:, head_cols(h, 0)] = dot(ds, k).astype(BF16)
        gproj[:, head_cols(h, 1)] = dot(ds, q, 0, 0).astype(BF16)
        return c

    lax.fori_loop(0, heads, backward, 0)

    per = n // 2
    wide_cols = 256

    def finish(i, c):
        b = lax.rem(me // per + 1 + i, 2)
        rs = pl.ds(pl.multiple_of(b * half, half), half)

        def back_project(k, c2):
            cols = pl.ds(pl.multiple_of(k * wide_cols, wide_cols), wide_cols)
            gn[:, cols] = dot(gproj[rs, :], w[cols, :], 1, 1)
            return c2

        lax.fori_loop(0, width // wide_cols, back_project, 0)
        scaled = gn[...] * gain[...]
        xb = mixp[pl.ds(b * per, per)].reshape(half, width).astype(F32)
        ib = inv[rs, :]
        mean = jnp.mean(scaled * xb, axis=-1, keepdims=True)
        gb = ib * (scaled - xb * ib * ib * mean)
        gbs[pl.ds(b * per, per)] = gb.astype(BF16).reshape(per, cc, width)

        def send4(j, c2):
            peer = b * per + lax.rem(me + n - j, per)
            d = lax.rem(peer + n - me, n)

            @pl.when(peer != me)
            def _():
                remote(gbs.at[peer], gbr.at[me], s4, r4, d, peer).start()

            return c2

        lax.fori_loop(0, per, send4, 0)
        return c

    lax.fori_loop(0, 2, finish, 0)
    gbr[pl.ds(me, 1)] = gbs[pl.ds(me, 1)]

    def recv4(d, c):
        src = lax.rem(me + n - d, n)
        remote(gbs.at[src], gbr.at[src], s4, r4, d, src).wait_recv()
        return c

    lax.fori_loop(1, n, recv4, 0)

    for g in range(groups):
        ch = slice(g * group, (g + 1) * group)
        gb = gbr[:, ch, :]
        emb = emb_up[ch, :] + jnp.sum(gb.astype(F32), axis=0)
        emb_all[pl.ds(mypos, 1), ch, :] = emb[None]
        gg = gb.reshape(long, width)
        prod = jnp.where(same, dot(gg, tokens[g], 1, 1), 0.0)
        wide = jnp.sum(prod.reshape(rows, group, long), axis=0)
        mg = mix_out[g] + jnp.dot(wide, pick_f, precision=HIGH, preferred_element_type=F32)
        mg = jnp.concatenate([mg, jnp.zeros((group, 128 - group), F32)], axis=1)
        mix_all[pl.ds(mypos, 1), ch, :] = mg[None]

    def pos_copy(ref, ss, rs, q, slot, partner):
        return pltpu.make_async_remote_copy(
            src_ref=ref.at[slot], dst_ref=ref.at[slot], send_sem=ss.at[q], recv_sem=rs.at[q],
            device_id={"pos": partner},
        )

    def send_pos(q, c):
        partner = lax.rem(mypos + q, npos)
        pos_copy(emb_all, se, re, q, mypos, partner).start()
        pos_copy(mix_all, sm, rm, q, mypos, partner).start()
        return c

    lax.fori_loop(1, npos, send_pos, 0)

    for g in range(groups):
        ch = slice(g * group, (g + 1) * group)
        gg = gbr[:, ch, :].reshape(long, width)
        gt = (gtok[g] + dot(block_diag(g), gg, 0, 0)).astype(BF16)
        pg = patches[:, 0, ch, :].reshape(long, pix)
        tok_out[0, g] = dot(pg, gt, 0, 0)

    def recv_pos(q, c):
        src = lax.rem(mypos + npos - q, npos)
        pos_copy(emb_all, se, re, q, src, src).wait_recv()
        pos_copy(mix_all, sm, rm, q, src, src).wait_recv()
        return c

    lax.fori_loop(1, npos, recv_pos, 0)
    emb_out[...] = jnp.sum(emb_all[...], axis=0)
    mix_sum = jnp.sum(mix_all[...], axis=0)
    for g in range(groups):
        mix_out[g] = mix_sum[g * group:(g + 1) * group, :group]

    own_enc.wait()

    def drain(d, c):
        peer = lax.rem(me + d, n)
        src = lax.rem(me + n - d, n)
        remote(encs.at[src], enc_out.at[src, 0], s3, r3, d, src).wait_recv()
        remote(mixed.at[peer], mixp.at[me], s1, r1, d, peer).wait_send()
        remote(up_hbm.at[peer, 0], upp.at[me], s2, r2, d, peer).wait_send()
        remote(encs.at[peer], enc_out.at[me, 0], s3, r3, d, peer).wait_send()
        remote(gbs.at[peer], gbr.at[me], s4, r4, d, peer).wait_send()
        return c

    lax.fori_loop(1, n, drain, 0)

    def drain_pos(q, c):
        partner = lax.rem(mypos + q, npos)
        pos_copy(emb_all, se, re, q, mypos, partner).wait_send()
        pos_copy(mix_all, sm, rm, q, mypos, partner).wait_send()
        return c

    lax.fori_loop(1, npos, drain_pos, 0)


def local(n, npos, patches, tok_weight, mixing, chan_embed, norm_gain, qkv_weight, upstream):
    rows, _, cc, _ = patches.shape
    groups, pix, width = tok_weight.shape
    group = mixing.shape[1]
    chans = n * cc
    heads = width // HDIM
    vm = functools.partial(pl.BlockSpec, memory_space=pltpu.VMEM)
    anyspace = pl.BlockSpec(memory_space=pl.ANY)
    dma = pltpu.SemaphoreType.DMA
    out_shape = (
        jax.ShapeDtypeStruct((rows, 1, cc, width), BF16),
        jax.ShapeDtypeStruct((1, groups, pix, width), F32),
        jax.ShapeDtypeStruct((groups, group, group), F32),
        jax.ShapeDtypeStruct((cc, width), F32),
    )
    block = pltpu.VMEM((n, cc, width), BF16)
    scratch = [
        pltpu.VMEM((groups, rows * group, width), BF16),
        block, block, block, block,
        pltpu.VMEM(qkv_weight.shape, BF16),
        pltpu.VMEM((chans, 3 * width), BF16),
        pltpu.VMEM((heads, chans, chans), F32),
        pltpu.VMEM((chans, 1), F32),
        block,
        pltpu.VMEM((chans, 3 * width), BF16),
        pltpu.VMEM((chans // 2, width), F32),
        block, block,
        pltpu.VMEM((npos, cc, width), F32),
        pltpu.VMEM((npos, groups * group, 128), F32),
        pltpu.VMEM((groups, rows * group, width), F32),
        pltpu.VMEM((cc, width), F32),
    ] + [dma((n,))] * 8 + [dma((npos,))] * 4 + [dma((4,))]
    return pl.pallas_call(
        functools.partial(kernel, n, npos),
        out_shape=out_shape,
        in_specs=[vm()] * 5 + [anyspace] * 2,
        out_specs=(anyspace, vm(), vm(), vm()),
        scratch_shapes=scratch,
        compiler_params=pltpu.CompilerParams(
            collective_id=0, has_side_effects=True, vmem_limit_bytes=56 * 1024 * 1024
        ),
    )(patches, tok_weight, mixing, chan_embed, norm_gain.reshape(1, width), qkv_weight, upstream)


def solution(mesh):
    in_specs = (
        P(None, "pos", "chan", None),
        P("chan", None, None),
        P("chan", None, None),
        P("chan", None),
        P(),
        P(),
        P(None, "pos", "chan", None),
    )
    out_specs = (
        P(None, "pos", "chan", None),
        P("pos", "chan", None, None),
        P("chan", None, None),
        P("chan", None),
    )
    body = functools.partial(local, mesh.shape["chan"], mesh.shape["pos"])
    return jax.shard_map(body, mesh=mesh, in_specs=in_specs, out_specs=out_specs, check_vma=False)
```
